512 devices in a mesh: slab: 16 (over z), head: 8 (over y, core), seq: 4 (over x).
Axes of the slice: x: 4, y: 4, z: 16, core: 2. Of those that a mesh axis runs over, the one named last changes fastest.
Arguments:
- qkv: bfloat16 [3, 64, 384, 4096], P(None, ('slab', 'seq'), 'head'), may hold values from -6 to 6
- pattern: int32 [64, 5], P('slab'), may hold values from 0 to 1, as said below
- counts: int32 [16], replicated, may hold values from 1 to 4, as said below
Outputs:
- attended: bfloat16 [64, 384, 4096], P(('slab', 'seq'), 'head')
The draws below stay inside these ranges and needn't reach their ends.
Inputs may be any that keep to these rules, and one draw needn't show every extreme that they name: Slab s holds counts[s] live tiles, in slots 0 to counts[s] - 1 of its 4; in every draw one slab holds 4 and one holds 1. `pattern`: the first tile of every slab has 1 in columns 3 and 4.
All inputs are finite; a program needn't handle non-finite values.
Results may differ from the reference program's by a relative error of at most 0.0049.
Values may be sent and summed in bfloat16 or wider, within the bound.
No kernel may reach another device: no remote copies, remote signals or barrier semaphores. Data moves between devices by JAX's collectives and lax.ppermute only.
A program may use at most 64 MiB of HBM per device.

```python
import math
import jax
import jax.numpy as jnp
from jax import lax

HEAD_DIM = 128
HEADS = 32
FEAT = 4096
TILE = 384
TPD = 1
GROUPS = 4
CAP = 4
TILES = 64


def draw_qkv(key, part):
    key = jax.random.fold_in(key, 7)
    base_key = jax.random.fold_in(key, 0)
    full_shape = (3, TILES, TILE, FEAT)
    spread = jnp.array([1.6, 1.6, 1.0], jnp.float32).reshape(3, 1, 1, 1)
    values = jax.random.truncated_normal(base_key, -3.75, 3.75, full_shape, jnp.float32) * spread
    return values.astype(jnp.bfloat16)


def draw_pattern(key, part):
    key = jax.random.fold_in(key, 13)
    values = jax.random.randint(key, (TILES, TPD + 4), 0, 2)
    firsts = jnp.arange(TILES // CAP, dtype=jnp.int32) * CAP
    values = values.at[firsts, TPD + 2].set(1).at[firsts, TPD + 3].set(1)
    return values.astype(jnp.int32)


def draw_counts(key, part):
    key = jax.random.fold_in(key, 11)
    pick_key, order_key = jax.random.split(key)
    slab_total = TILES // CAP
    values = jax.random.randint(pick_key, (slab_total,), TPD, CAP + 1)
    shuffled = jax.random.permutation(order_key, slab_total)
    values = values.at[shuffled[0]].set(CAP).at[shuffled[1]].set(TPD)
    return values.astype(jnp.int32)


def setup_inputs(seed: int = 0) -> dict:
    key_of = jax.random.split(jax.random.key(seed), 4)
    return {
        "qkv": draw_qkv(jax.random.fold_in(key_of[3], 71), 0),
        "pattern": draw_pattern(jax.random.fold_in(key_of[3], 71), 0),
        "counts": draw_counts(jax.random.fold_in(key_of[3], 71), 0),
    }


def pick_count(counts, slab_rows):
    slab_ids = jnp.arange(counts.shape[0], dtype=jnp.int32)
    return lax.optimization_barrier(jnp.sum(jnp.where(slab_rows[..., None] == slab_ids, counts, 0), axis=-1))

def tile_plan(pattern_rows, counts, slab_rows, group_ids, places, group_total, per_group):
    slab_total = counts.shape[0]
    first_slot = group_ids * per_group
    same_slab = jnp.zeros_like(first_slot) + slab_rows
    always = jnp.ones(first_slot.shape, dtype=bool)
    slot_list = [first_slot + offset for offset in range(per_group)]
    slot_list = slot_list + [first_slot - 1, first_slot + per_group, first_slot + per_group - 1, first_slot]
    slab_list = [same_slab] * (per_group + 2) + [same_slab - 1, same_slab + 1]
    exist_list = [always] * per_group + [group_ids >= 1, group_ids + 1 < group_total, same_slab >= 1, same_slab + 1 < slab_total]
    key_slot = jnp.stack(slot_list, axis=1)
    key_slab = jnp.stack(slab_list, axis=1)
    exists = jnp.stack(exist_list, axis=1)
    live_key = exists & (key_slot < pick_count(counts, key_slab))
    columns = jnp.arange(per_group + 4, dtype=jnp.int32)
    allowed = ((pattern_rows == 1) | (columns[None, :] == places[:, None])) & live_key
    live_query = first_slot + places < pick_count(counts, same_slab)
    return (allowed, live_query, key_slab, key_slot)

def attend(query_rows, key_rows, value_rows, allowed, live_query):
    per_group, cand_count = allowed.shape
    tile_len = query_rows.shape[0] // per_group
    score_scale = 1.0 / math.sqrt(query_rows.shape[-1])
    scores = jnp.einsum('qd,kd->qk', query_rows, key_rows, preferred_element_type=jnp.float32) * score_scale
    scores = scores.reshape(per_group, tile_len, cand_count, tile_len)
    usable = allowed[:, None, :, None]
    peak_score = lax.optimization_barrier(jnp.max(jnp.where(usable, scores, -1e+30), axis=(2, 3), keepdims=True))
    weights = jnp.where(usable, jnp.exp(scores - peak_score), 0.0)
    totals = lax.optimization_barrier(jnp.sum(weights, axis=(2, 3), keepdims=True))
    totals = jnp.where(live_query[:, None, None, None], totals, 1.0)
    shares = (weights / totals).astype(jnp.bfloat16).reshape(per_group * tile_len, cand_count * tile_len)
    mixed_out = jnp.dot(shares.astype(value_rows.dtype), value_rows, preferred_element_type=jnp.float32)
    mixed_out = mixed_out.reshape(per_group, tile_len, -1)
    mixed_out = jnp.where(live_query[:, None, None], mixed_out, 0.0)
    return mixed_out.astype(jnp.bfloat16).reshape(per_group * tile_len, -1)

def reference(qkv, pattern, counts):
    tile_ids = jnp.arange(TILES, dtype=jnp.int32)
    slot_ids = tile_ids % CAP
    group_ids = slot_ids // TPD
    places = slot_ids % TPD
    slab_rows = tile_ids // CAP
    allowed, live_query, key_slab, key_slot = tile_plan(pattern, counts, slab_rows, group_ids, places, GROUPS, TPD)
    key_tile = jnp.clip(key_slab * CAP + key_slot, 0, TILES - 1).astype(jnp.int32)
    group_total = TILES // TPD
    group_keys = key_tile.reshape(group_total, TPD, TPD + 4)[:, 0]
    group_allowed = allowed.reshape(group_total, TPD, TPD + 4)
    group_live = live_query.reshape(group_total, TPD)

    def one_group(group_index):
        start = (group_index * TPD).astype(jnp.int32)
        queries = lax.dynamic_slice_in_dim(qkv, start, TPD, 1)[0]
        queries = queries.astype(jnp.float32).reshape(TPD * TILE, HEADS, HEAD_DIM)
        picked = jnp.take(qkv, group_keys[group_index], axis=1)
        key_rows = picked[1].astype(jnp.float32).reshape((TPD + 4) * TILE, HEADS, HEAD_DIM)
        value_rows = picked[2].astype(jnp.float32).reshape((TPD + 4) * TILE, HEADS, HEAD_DIM)
        per_head = jax.vmap(attend, in_axes=(1, 1, 1, None, None), out_axes=1)(queries, key_rows, value_rows, group_allowed[group_index], group_live[group_index])
        return per_head.reshape(TPD, TILE, FEAT)
    attended = lax.map(one_group, jnp.arange(group_total, dtype=jnp.int32))
    return attended.reshape(TILES, TILE, FEAT)
```

```python
import functools
import math

import jax
import jax.numpy as jnp
from jax import lax
from jax.experimental import pallas as pl
from jax.experimental.pallas import tpu as pltpu
from jax.sharding import PartitionSpec as P

HEAD_DIM = 128
BLOCKED = -1e30
PLANE = ("seq", "head")


def swap_pairs(value, axis, first):
    length = lax.axis_size(axis)
    pairs = []
    for low in range(first, length - 1, 2):
        pairs += [(low, low + 1), (low + 1, low)]
    return lax.ppermute(value, axis, pairs)


def to_blocks(rows, parts):
    split = rows.reshape(*rows.shape[:-1], parts, rows.shape[-1] // parts)
    return jnp.moveaxis(split, -2, 0)


def spread(blocks):
    return lax.all_to_all(blocks, PLANE, split_axis=0, concat_axis=0, tiled=True)


def attend_kernel(slab_ref, pattern_ref, counts_ref, q_ref, own_ref, even_ref, odd_ref, out_ref):
    tiles, pieces, piece, width = q_ref.shape
    tile_len = pieces * piece
    slab_total = counts_ref.shape[0]
    scale = math.log2(math.e) / math.sqrt(HEAD_DIM)
    slab = slab_ref[0]
    here = counts_ref[slab]
    even_slab = slab + 1 - 2 * lax.rem(slab, 2)
    odd_slab = slab - 1 + 2 * lax.rem(slab, 2)

    def live_in(other):
        count = counts_ref[jnp.clip(other, 0, slab_total - 1)]
        return jnp.where((other >= 0) & (other < slab_total), count, 0)

    even_count, odd_count = live_in(even_slab), live_in(odd_slab)
    even_column = jnp.where(even_slab < slab, 3, 4)
    odd_column = jnp.where(odd_slab < slab, 3, 4)

    for tile in range(tiles):
        live = tile < here
        asked = [(own_ref, tile, live)]
        if tile >= 1:
            asked.append((own_ref, tile - 1, (pattern_ref[tile, 1] == 1) & (tile - 1 < here)))
        if tile + 1 < tiles:
            asked.append((own_ref, tile + 1, (pattern_ref[tile, 2] == 1) & (tile + 1 < here)))
        asked.append((even_ref, tile, (pattern_ref[tile, even_column] == 1) & (tile < even_count)))
        asked.append((odd_ref, tile, (pattern_ref[tile, odd_column] == 1) & (tile < odd_count)))

        @pl.when(live)
        def _():
            query = q_ref[tile].reshape(tile_len, width)
            scores, peaks, biases = [], [], []
            for ref, place, allowed in asked:
                key = ref[place, :, 0].reshape(tile_len, width)
                score = lax.dot_general(
                    query, key, (((1,), (1,)), ((), ())), preferred_element_type=jnp.float32
                )
                bias = jnp.where(allowed, 0.0, BLOCKED)
                scores.append(score)
                biases.append(bias)
                peaks.append(jnp.max(score, axis=1, keepdims=True) + bias)
            peak = functools.reduce(jnp.maximum, peaks)
            total = jnp.zeros((tile_len, 1), jnp.float32)
            mixed = jnp.zeros((tile_len, width), jnp.float32)
            for score, bias, (ref, place, _) in zip(scores, biases, asked):
                weight = jnp.exp2(score * scale + (bias - peak) * scale)
                total += jnp.sum(weight, axis=1, keepdims=True)
                value = ref[place, :, 1].reshape(tile_len, width)
                mixed += jnp.dot(
                    weight.astype(jnp.bfloat16), value, preferred_element_type=jnp.float32
                )
            out_ref[tile] = (mixed / total).astype(jnp.bfloat16).reshape(pieces, piece, width)

        @pl.when(jnp.logical_not(live))
        def _():
            out_ref[tile] = jnp.zeros((pieces, piece, width), jnp.bfloat16)


def on_device(qkv, pattern, counts):
    seq_count, head_count = lax.axis_size("seq"), lax.axis_size("head")
    parts = seq_count * head_count
    piece, features = qkv.shape[2], qkv.shape[3]
    width = features // parts
    own = spread(to_blocks(qkv[1:3, 0], parts))
    own, raw_query = lax.optimization_barrier((own, qkv[0, 0]))
    own = own.reshape(seq_count, head_count, 2, piece, width)
    even = swap_pairs(own, "slab", 0)
    odd = swap_pairs(own, "slab", 1)
    query = spread(to_blocks(raw_query, parts)).reshape(seq_count, head_count, piece, width)
    slab = lax.axis_index("slab").astype(jnp.int32).reshape(1)
    smem = pl.BlockSpec(memory_space=pltpu.SMEM)
    vmem = pl.BlockSpec(memory_space=pltpu.VMEM)
    pairs = seq_count * 5 * (head_count * piece) ** 2
    attended = pl.pallas_call(
        attend_kernel,
        out_shape=jax.ShapeDtypeStruct(query.shape, jnp.bfloat16),
        in_specs=[smem] * 3 + [vmem] * 4,
        out_specs=vmem,
        compiler_params=pltpu.CompilerParams(vmem_limit_bytes=48 * 2**20),
        cost_estimate=pl.CostEstimate(
            flops=4 * width * pairs, bytes_accessed=8 * query.size * 2, transcendentals=pairs
        ),
    )(slab, pattern, counts, query, own, even, odd)
    returned = spread(attended.reshape(parts, piece, width))
    return jnp.moveaxis(returned, 0, 1).reshape(1, piece, features)


def solution(mesh):
    in_specs = (P(None, ("slab", "seq"), "head", None), P("slab", None), P())
    out_specs = P(("slab", "seq"), "head", None)
    return jax.shard_map(
        on_device, mesh=mesh, in_specs=in_specs, out_specs=out_specs, check_vma=False
    )
```

```python
import functools
import math

import jax
import jax.numpy as jnp
from jax import lax
from jax.experimental import pallas as pl
from jax.experimental.pallas import tpu as pltpu
from jax.sharding import PartitionSpec as P

HEAD_DIM = 128
BLOCKED = -1e30
SCALE = math.log2(math.e) / math.sqrt(HEAD_DIM)
SMEM = pl.BlockSpec(memory_space=pltpu.SMEM)
VMEM = pl.BlockSpec(memory_space=pltpu.VMEM)
PARAMS = pltpu.CompilerParams(vmem_limit_bytes=40 * 2**20)


def passed_along(value, axis, even_by):
    length, heads = lax.axis_size(axis), lax.axis_size("head")
    outer = axis == "slab"
    pairs = []
    for place in range(length):
        for head in range(heads):
            target = place + (even_by if head % 2 == 0 else -even_by)
            if 0 <= target < length:
                if outer:
                    pairs.append((place * heads + head, target * heads + head))
                else:
                    pairs.append((head * length + place, head * length + target))
    return lax.ppermute(value, (axis, "head") if outer else ("head", axis), pairs)


def spread(blocks):
    return lax.all_to_all(blocks, "head", split_axis=0, concat_axis=0, tiled=True)


def to_blocks_kernel(rows_ref, blocks_ref):
    parts, arrays, _, width = blocks_ref.shape
    for array in range(arrays):
        for part in range(parts):
            columns = slice(part * width, (part + 1) * width)
            blocks_ref[part, array] = rows_ref[array, 0, :, columns]


def to_blocks(rows, parts):
    arrays, _, tokens, features = rows.shape
    return pl.pallas_call(
        to_blocks_kernel,
        out_shape=jax.ShapeDtypeStruct((parts, arrays, tokens, features // parts), rows.dtype),
        in_specs=[VMEM],
        out_specs=VMEM,
        compiler_params=PARAMS,
        cost_estimate=pl.CostEstimate(flops=0, bytes_accessed=4 * rows.size, transcendentals=0),
    )(rows)


def to_rows_kernel(blocks_ref, rows_ref):
    parts, _, width = blocks_ref.shape
    for part in range(parts):
        rows_ref[0, :, part * width : (part + 1) * width] = blocks_ref[part]


def to_rows(blocks):
    parts, tokens, width = blocks.shape
    return pl.pallas_call(
        to_rows_kernel,
        out_shape=jax.ShapeDtypeStruct((1, tokens, parts * width), blocks.dtype),
        in_specs=[VMEM],
        out_specs=VMEM,
        compiler_params=PARAMS,
        cost_estimate=pl.CostEstimate(flops=0, bytes_accessed=4 * blocks.size, transcendentals=0),
    )(blocks)


def columns_of(ref, which, head):
    pieces, _, piece, _ = ref.shape
    columns = slice(head * HEAD_DIM, (head + 1) * HEAD_DIM)
    return ref[:, which, :, columns].reshape(pieces * piece, HEAD_DIM)


def attend_kernel(place_ref, pattern_ref, counts_ref, q_ref, own_ref, x1_ref, z1_ref, x0_ref, z0_ref, out_ref):
    pieces, _, piece, width = q_ref.shape
    tile_len = pieces * piece
    last = counts_ref.shape[0] - 1
    slab, slot, core = place_ref[0], place_ref[1], place_ref[2]
    here = counts_ref[slab]
    below = jnp.where(slab >= 1, counts_ref[jnp.maximum(slab - 1, 0)], 0)
    above = jnp.where(slab < last, counts_ref[jnp.minimum(slab + 1, last)], 0)
    wants = [pattern_ref[slot, column] == 1 for column in range(5)]
    left = wants[1] & (slot >= 1)
    right = wants[2] & (slot + 1 < here)
    down = wants[3] & (slot < below)
    up = wants[4] & (slot < above)
    even = core == 0
    asked = [
        (own_ref, True),
        (x0_ref, (even & left) | (~even & right)),
        (x1_ref, (even & right) | (~even & left)),
        (z0_ref, (even & down) | (~even & up)),
        (z1_ref, (even & up) | (~even & down)),
    ]
    biases = [jnp.where(allowed, 0.0, BLOCKED) for _, allowed in asked]

    @pl.when(slot < here)
    def _():
        for head in range(width // HEAD_DIM):
            query = columns_of(q_ref, 0, head)
            scores = [
                lax.dot_general(
                    query,
                    columns_of(ref, 0, head),
                    (((1,), (1,)), ((), ())),
                    preferred_element_type=jnp.float32,
                )
                for ref, _ in asked
            ]
            tops = [
                functools.reduce(
                    jnp.maximum, [score[:, k : k + 128] for k in range(0, tile_len, 128)]
                )
                + bias
                for score, bias in zip(scores, biases)
            ]
            peak = jnp.max(functools.reduce(jnp.maximum, tops), axis=1, keepdims=True)
            total, mixed = 0.0, 0.0
            for score, bias, (ref, _) in zip(scores, biases, asked):
                weight = jnp.exp2(score * SCALE + (bias - peak) * SCALE)
                total += functools.reduce(
                    jnp.add, [weight[:, k : k + 128] for k in range(0, tile_len, 128)]
                )
                mixed += jnp.dot(
                    weight.astype(jnp.bfloat16),
                    columns_of(ref, 1, head),
                    preferred_element_type=jnp.float32,
                )
            mixed = mixed / jnp.sum(total, axis=1, keepdims=True)
            out_ref[:, :, head * HEAD_DIM : (head + 1) * HEAD_DIM] = mixed.astype(
                jnp.bfloat16
            ).reshape(pieces, piece, HEAD_DIM)

    @pl.when(slot >= here)
    def _():
        out_ref[...] = jnp.zeros(out_ref.shape, jnp.bfloat16)


def on_device(qkv, pattern, counts):
    parts = lax.axis_size("head")
    piece, features = qkv.shape[2], qkv.shape[3]
    width = features // parts
    place = jnp.stack(
        [lax.axis_index("slab"), lax.axis_index("seq"), lax.axis_index("head") % 2]
    ).astype(jnp.int32)
    own = spread(to_blocks(qkv[1:3], parts))
    own, raw_query = lax.optimization_barrier((own, to_blocks(qkv[:1], parts)))
    z0 = passed_along(own, "slab", 1)
    x0 = passed_along(own, "seq", 1)
    z1 = passed_along(own, "slab", -1)
    x1 = passed_along(own, "seq", -1)
    query = spread(raw_query)
    attended = pl.pallas_call(
        attend_kernel,
        out_shape=jax.ShapeDtypeStruct((parts, piece, width), jnp.bfloat16),
        in_specs=[SMEM] * 3 + [VMEM] * 6,
        out_specs=VMEM,
        compiler_params=PARAMS,
        cost_estimate=pl.CostEstimate(
            flops=1500000000, bytes_accessed=2**22, transcendentals=2949120
        ),
    )(place, pattern, counts, query, own, x1, z1, x0, z0)
    return to_rows(spread(attended))


def solution(mesh):
    in_specs = (P(None, ("slab", "seq"), "head", None), P("slab", None), P())
    out_specs = P(("slab", "seq"), "head", None)
    return jax.shard_map(
        on_device, mesh=mesh, in_specs=in_specs, out_specs=out_specs, check_vma=False
    )
```

```python
import functools
import math

import jax
import jax.numpy as jnp
from jax import lax
from jax.experimental import pallas as pl
from jax.experimental.pallas import tpu as pltpu
from jax.sharding import Mesh
from jax.sharding import PartitionSpec as P

HEAD_DIM = 128
PAIR = ("lane", "head")
SCALE = math.log2(math.e) / math.sqrt(HEAD_DIM)
SMEM = pl.BlockSpec(memory_space=pltpu.SMEM)
VMEM = pl.BlockSpec(memory_space=pltpu.VMEM)
PARAMS = pltpu.CompilerParams(vmem_limit_bytes=40 * 2**20)


def passed_along(value, even_by):
    slabs, heads = lax.axis_size("slab"), lax.axis_size("head")
    moves = []
    for slab in range(slabs):
        for head in range(heads):
            target = slab + (even_by if head % 2 == 0 else -even_by)
            if 0 <= target < slabs:
                moves.append((slab * heads + head, target * heads + head))
    return lax.ppermute(value, ("slab", "head"), moves)


def swapped_across(value):
    return lax.ppermute(value, ("pair", "lane"), [(0, 3), (3, 0), (1, 2), (2, 1)])


def spread(blocks):
    return lax.all_to_all(blocks, PAIR, split_axis=0, concat_axis=0, tiled=True)


def each_pair(move):
    for pair in range(2):
        pl.when(lax.axis_index("pair") == pair)(functools.partial(move, pair))


def to_blocks_kernel(rows_ref, blocks_ref):
    parts, arrays, _, width = blocks_ref.shape

    def move(pair):
        for array in range(arrays):
            for part in range(parts):
                source = (part + pair * parts // 2) % parts
                columns = slice(source * width, (source + 1) * width)
                blocks_ref[part, array] = rows_ref[array, 0, :, columns]

    each_pair(move)


def to_blocks(rows, parts):
    arrays, _, tokens, features = rows.shape
    return pl.pallas_call(
        to_blocks_kernel,
        out_shape=jax.ShapeDtypeStruct((parts, arrays, tokens, features // parts), rows.dtype),
        in_specs=[VMEM],
        out_specs=VMEM,
        compiler_params=PARAMS,
        cost_estimate=pl.CostEstimate(flops=0, bytes_accessed=4 * rows.size, transcendentals=0),
    )(rows)


def to_rows_kernel(blocks_ref, rows_ref):
    parts, _, width = blocks_ref.shape

    def move(pair):
        for part in range(parts):
            target = (part + pair * parts // 2) % parts
            rows_ref[0, :, target * width : (target + 1) * width] = blocks_ref[part]

    each_pair(move)


def to_rows(blocks):
    parts, tokens, width = blocks.shape
    return pl.pallas_call(
        to_rows_kernel,
        out_shape=jax.ShapeDtypeStruct((1, tokens, parts * width), blocks.dtype),
        in_specs=[VMEM],
        out_specs=VMEM,
        compiler_params=PARAMS,
        cost_estimate=pl.CostEstimate(flops=0, bytes_accessed=4 * blocks.size, transcendentals=0),
    )(blocks)


def columns_of(pieces, head):
    rows = pieces[:, :, head * HEAD_DIM : (head + 1) * HEAD_DIM]
    return rows.reshape(rows.shape[0] * rows.shape[1], HEAD_DIM)


def key_of(place, head):
    ref, tile = place
    return columns_of(ref.at[tile, :, 0], head)


def value_of(place, head):
    ref, tile = place
    return columns_of(ref.at[tile, :, 1], head)


def lanes(op, score):
    return functools.reduce(
        op, [score[:, k : k + HEAD_DIM] for k in range(0, score.shape[1], HEAD_DIM)]
    )


def score(query, key):
    return lax.dot_general(query, key, (((1,), (1,)), ((), ())), preferred_element_type=jnp.float32)


def attend(q_ref, out_ref, tile, places):
    _, pieces, piece, width = out_ref.shape
    heads = range(width // HEAD_DIM)
    queries = [columns_of(q_ref.at[tile], head) for head in heads]
    ready = [score(queries[0], key_of(place, 0)) for place in places]
    for head in heads:
        scores, ready = ready, []
        top = functools.reduce(jnp.maximum, [lanes(jnp.maximum, one) for one in scores])
        shift = jnp.max(top, axis=1, keepdims=True) * SCALE
        total, mixed = 0.0, 0.0
        for one, place in zip(scores, places):
            weight = jnp.exp2(one * SCALE - shift)
            total += lanes(jnp.add, weight)
            if head + 1 < len(heads):
                ready.append(score(queries[head + 1], key_of(place, head + 1)))
            mixed += jnp.dot(
                weight.astype(jnp.bfloat16),
                value_of(place, head),
                preferred_element_type=jnp.float32,
            )
        mixed = mixed / jnp.sum(total, axis=1, keepdims=True)
        columns = slice(head * HEAD_DIM, (head + 1) * HEAD_DIM)
        out_ref[tile, :, :, columns] = mixed.astype(jnp.bfloat16).reshape(pieces, piece, HEAD_DIM)


def attend_kernel(pattern_ref, counts_ref, q_ref, own_ref, x_ref, z1_ref, z0_ref, out_ref):
    tiles = out_ref.shape[0]
    last = counts_ref.shape[0] - 1
    slab, pair = lax.axis_index("slab"), lax.axis_index("pair")
    core = lax.rem(lax.axis_index("head"), 2)
    here = counts_ref[slab]
    below = jnp.where(slab >= 1, counts_ref[jnp.maximum(slab - 1, 0)], 0)
    above = jnp.where(slab < last, counts_ref[jnp.minimum(slab + 1, last)], 0)

    @pl.loop(0, tiles)
    def _(tile):
        slot = tiles * pair + tile
        live = slot < here
        left = pattern_ref[slot, 1] == 1
        right = (pattern_ref[slot, 2] == 1) & (slot + 1 < here)
        down = (pattern_ref[slot, 3] == 1) & (slot < below)
        up = (pattern_ref[slot, 4] == 1) & (slot < above)
        inner, outer = (tile == 0, tile == 1)
        others = [
            ((own_ref, 1 - tile), (inner & right) | (outer & left)),
            ((x_ref, 0), (pair != tile) & ((inner & left) | (outer & right))),
            ((z0_ref, tile), ((core == 0) & down) | ((core == 1) & up)),
            ((z1_ref, tile), ((core == 0) & up) | ((core == 1) & down)),
        ]
        code = sum(jnp.where(allowed, 1 << k, 0) for k, (_, allowed) in enumerate(others))
        for subset in range(1 << len(others)):
            places = [(own_ref, tile)]
            places += [place for k, (place, _) in enumerate(others) if subset >> k & 1]
            pl.when(live & (code == subset))(
                functools.partial(attend, q_ref, out_ref, tile, places)
            )

        @pl.when(jnp.logical_not(live))
        def _():
            out_ref[tile] = jnp.zeros(out_ref.shape[1:], jnp.bfloat16)


def on_device(qkv, pattern, counts):
    pair_len, heads = lax.axis_size("lane"), lax.axis_size("head")
    parts = pair_len * heads
    piece, features = qkv.shape[2], qkv.shape[3]
    width = features // parts
    pair = lax.axis_index("pair")
    own = spread(to_blocks(qkv[1:3], parts))
    own, raw_query = lax.optimization_barrier((own, to_blocks(qkv[:1], parts)))
    own = own.reshape(pair_len, heads, 2, piece, width)
    z0 = passed_along(own, 1)
    z1 = passed_along(own, -1)
    x = swapped_across(lax.dynamic_slice_in_dim(own, 1 - pair, 1, axis=0))
    query = spread(raw_query).reshape(pair_len, heads, piece, width)
    attended = pl.pallas_call(
        attend_kernel,
        out_shape=jax.ShapeDtypeStruct(query.shape, jnp.bfloat16),
        in_specs=[SMEM] * 2 + [VMEM] * 5,
        out_specs=VMEM,
        compiler_params=PARAMS,
        cost_estimate=pl.CostEstimate(flops=10**9, bytes_accessed=2**22, transcendentals=0),
    )(pattern, counts, query, own, x, z1, z0)
    return to_rows(spread(attended.reshape(parts, piece, width)))


def solution(mesh):
    slabs, heads, slots = (mesh.shape[axis] for axis in ("slab", "head", "seq"))
    halves = Mesh(mesh.devices.reshape(slabs, heads, 2, slots // 2), ("slab", "head", "pair", "lane"))
    in_specs = (P(None, ("slab", "pair", "lane"), "head", None), P("slab", None), P())
    out_specs = P(("slab", "pair", "lane"), "head", None)
    return jax.shard_map(
        on_device, mesh=halves, in_specs=in_specs, out_specs=out_specs, check_vma=False
    )
```

```python
import functools
import math

import jax
import jax.numpy as jnp
from jax import lax
from jax.experimental import pallas as pl
from jax.experimental.pallas import tpu as pltpu
from jax.sharding import Mesh
from jax.sharding import PartitionSpec as P

HEAD_DIM = 128
PAIR = ("lane", "head")
SCALE = math.log2(math.e) / math.sqrt(HEAD_DIM)
SMEM = pl.BlockSpec(memory_space=pltpu.SMEM)
VMEM = pl.BlockSpec(memory_space=pltpu.VMEM)
PARAMS = pltpu.CompilerParams(vmem_limit_bytes=40 * 2**20)


def passed_along(value, even_by):
    slabs, heads = lax.axis_size("slab"), lax.axis_size("head")
    moves = []
    for slab in range(slabs):
        for head in range(heads):
            target = slab + (even_by if head % 2 == 0 else -even_by)
            if 0 <= target < slabs:
                moves.append((slab * heads + head, target * heads + head))
    return lax.ppermute(value, ("slab", "head"), moves)


def swapped_across(value):
    return lax.ppermute(value, ("pair", "lane"), [(0, 3), (3, 0), (1, 2), (2, 1)])


def spread(blocks):
    return lax.all_to_all(blocks, PAIR, split_axis=0, concat_axis=0, tiled=True)


def each_pair(move):
    for pair in range(2):
        pl.when(lax.axis_index("pair") == pair)(functools.partial(move, pair))


def to_blocks_kernel(rows_ref, blocks_ref):
    parts, arrays, _, width = blocks_ref.shape

    def move(pair):
        for array in range(arrays):
            for part in range(parts):
                source = (part + pair * parts // 2) % parts
                columns = slice(source * width, (source + 1) * width)
                blocks_ref[part, array] = rows_ref[array, 0, :, columns]

    each_pair(move)


def to_blocks(rows, parts):
    arrays, _, tokens, features = rows.shape
    return pl.pallas_call(
        to_blocks_kernel,
        out_shape=jax.ShapeDtypeStruct((parts, arrays, tokens, features // parts), rows.dtype),
        in_specs=[VMEM],
        out_specs=VMEM,
        compiler_params=PARAMS,
        cost_estimate=pl.CostEstimate(flops=0, bytes_accessed=4 * rows.size, transcendentals=0),
    )(rows)


def to_rows_kernel(blocks_ref, rows_ref):
    parts, _, width = blocks_ref.shape

    def move(pair):
        for part in range(parts):
            target = (part + pair * parts // 2) % parts
            rows_ref[0, :, target * width : (target + 1) * width] = blocks_ref[part]

    each_pair(move)


def to_rows(blocks):
    parts, tokens, width = blocks.shape
    return pl.pallas_call(
        to_rows_kernel,
        out_shape=jax.ShapeDtypeStruct((1, tokens, parts * width), blocks.dtype),
        in_specs=[VMEM],
        out_specs=VMEM,
        compiler_params=PARAMS,
        cost_estimate=pl.CostEstimate(flops=0, bytes_accessed=4 * blocks.size, transcendentals=0),
    )(blocks)


def columns_of(pieces, head):
    rows = pieces[:, :, head * HEAD_DIM : (head + 1) * HEAD_DIM]
    return rows.reshape(rows.shape[0] * rows.shape[1], HEAD_DIM)


def key_of(place, head):
    ref, tile = place
    return columns_of(ref.at[tile, :, 0], head)


def value_of(place, head):
    ref, tile = place
    return columns_of(ref.at[tile, :, 1], head)


def lanes(op, score):
    return functools.reduce(
        op, [score[:, k : k + HEAD_DIM] for k in range(0, score.shape[1], HEAD_DIM)]
    )


def score(query, key):
    return lax.dot_general(query, key, (((1,), (1,)), ((), ())), preferred_element_type=jnp.float32)


def attend(q_ref, out_ref, tile, places):
    _, pieces, piece, width = out_ref.shape
    heads = range(width // HEAD_DIM)
    queries = [columns_of(q_ref.at[tile], head) for head in heads]
    ready = [score(queries[0], key_of(place, 0)) for place in places]
    for head in heads:
        scores, ready = ready, []
        top = functools.reduce(jnp.maximum, [lanes(jnp.maximum, one) for one in scores])
        shift = jnp.max(top, axis=1, keepdims=True) * SCALE
        total, mixed = 0.0, 0.0
        for one, place in zip(scores, places):
            weight = jnp.exp2(one * SCALE - shift)
            total += lanes(jnp.add, weight)
            if head + 1 < len(heads):
                ready.append(score(queries[head + 1], key_of(place, head + 1)))
            mixed += jnp.dot(
                weight.astype(jnp.bfloat16),
                value_of(place, head),
                preferred_element_type=jnp.float32,
            )
        mixed = mixed / jnp.sum(total, axis=1, keepdims=True)
        columns = slice(head * HEAD_DIM, (head + 1) * HEAD_DIM)
        out_ref[tile, :, :, columns] = mixed.astype(jnp.bfloat16).reshape(pieces, piece, HEAD_DIM)


def attend_kernel(pattern_ref, counts_ref, q_ref, own_ref, x_ref, z1_ref, z0_ref, out_ref):
    tiles = out_ref.shape[0]
    last = counts_ref.shape[0] - 1
    slab, pair = lax.axis_index("slab"), lax.axis_index("pair")
    core = lax.rem(lax.axis_index("head"), 2)
    here = counts_ref[slab]
    below = jnp.where(slab >= 1, counts_ref[jnp.maximum(slab - 1, 0)], 0)
    above = jnp.where(slab < last, counts_ref[jnp.minimum(slab + 1, last)], 0)

    @pl.loop(0, tiles)
    def _(tile):
        slot = tiles * pair + tile
        live = slot < here
        left = pattern_ref[slot, 1] == 1
        right = (pattern_ref[slot, 2] == 1) & (slot + 1 < here)
        down = (pattern_ref[slot, 3] == 1) & (slot < below)
        up = (pattern_ref[slot, 4] == 1) & (slot < above)
        inner, outer = (tile == 0, tile == 1)
        others = [
            ((own_ref, 1 - tile), (inner & right) | (outer & left)),
            ((x_ref, 0), (pair != tile) & ((inner & left) | (outer & right))),
            ((z0_ref, tile), ((core == 0) & down) | ((core == 1) & up)),
            ((z1_ref, tile), ((core == 0) & up) | ((core == 1) & down)),
        ]
        def choose(k, places):
            if k == len(others):
                attend(q_ref, out_ref, tile, places)
                return
            place, allowed = others[k]
            pl.when(allowed)(lambda: choose(k + 1, places + [place]))
            pl.when(jnp.logical_not(allowed))(lambda: choose(k + 1, places))

        pl.when(live)(lambda: choose(0, [(own_ref, tile)]))

        @pl.when(jnp.logical_not(live))
        def _():
            out_ref[tile] = jnp.zeros(out_ref.shape[1:], jnp.bfloat16)


def on_device(qkv, pattern, counts):
    pair_len, heads = lax.axis_size("lane"), lax.axis_size("head")
    parts = pair_len * heads
    piece, features = qkv.shape[2], qkv.shape[3]
    width = features // parts
    pair = lax.axis_index("pair")
    own = spread(to_blocks(qkv[1:3], parts))
    own, raw_query = lax.optimization_barrier((own, to_blocks(qkv[:1], parts)))
    own = own.reshape(pair_len, heads, 2, piece, width)
    z0 = passed_along(own, 1)
    z1 = passed_along(own, -1)
    x = swapped_across(lax.dynamic_slice_in_dim(own, 1 - pair, 1, axis=0))
    query = spread(raw_query).reshape(pair_len, heads, piece, width)
    attended = pl.pallas_call(
        attend_kernel,
        out_shape=jax.ShapeDtypeStruct(query.shape, jnp.bfloat16),
        in_specs=[SMEM] * 2 + [VMEM] * 5,
        out_specs=VMEM,
        compiler_params=PARAMS,
        cost_estimate=pl.CostEstimate(flops=10**9, bytes_accessed=2**22, transcendentals=0),
    )(pattern, counts, query, own, x, z1, z0)
    return to_rows(spread(attended.reshape(parts, piece, width)))


def solution(mesh):
    slabs, heads, slots = (mesh.shape[axis] for axis in ("slab", "head", "seq"))
    halves = Mesh(mesh.devices.reshape(slabs, heads, 2, slots // 2), ("slab", "head", "pair", "lane"))
    in_specs = (P(None, ("slab", "pair", "lane"), "head", None), P("slab", None), P())
    out_specs = P(("slab", "pair", "lane"), "head", None)
    return jax.shard_map(
        on_device, mesh=halves, in_specs=in_specs, out_specs=out_specs, check_vma=False
    )
```

```python
import functools
import math

import jax
import jax.numpy as jnp
from jax import lax
from jax.experimental import pallas as pl
from jax.experimental.pallas import tpu as pltpu
from jax.sharding import Mesh
from jax.sharding import PartitionSpec as P

HEAD_DIM = 128
LARGE = 1e30
BLOCKED = -1e30
PAIR = ("lane", "head")
SCALE = math.log2(math.e) / math.sqrt(HEAD_DIM)
SMEM = pl.BlockSpec(memory_space=pltpu.SMEM)
VMEM = pl.BlockSpec(memory_space=pltpu.VMEM)
PARAMS = pltpu.CompilerParams(vmem_limit_bytes=40 * 2**20)


def passed_along(value, even_by):
    slabs, heads = lax.axis_size("slab"), lax.axis_size("head")
    moves = []
    for slab in range(slabs):
        for head in range(heads):
            target = slab + (even_by if head % 2 == 0 else -even_by)
            if 0 <= target < slabs:
                moves.append((slab * heads + head, target * heads + head))
    return lax.ppermute(value, ("slab", "head"), moves)


def swapped_across(value):
    return lax.ppermute(value, ("pair", "lane"), [(0, 3), (3, 0), (1, 2), (2, 1)])


def spread(blocks):
    return lax.all_to_all(blocks, PAIR, split_axis=0, concat_axis=0, tiled=True)


def each_pair(move):
    for pair in range(2):
        pl.when(lax.axis_index("pair") == pair)(functools.partial(move, pair))


def to_blocks_kernel(rows_ref, blocks_ref):
    parts, arrays, _, width = blocks_ref.shape

    def move(pair):
        for array in range(arrays):
            for part in range(parts):
                source = (part + pair * parts // 2) % parts
                columns = slice(source * width, (source + 1) * width)
                blocks_ref[part, array] = rows_ref[array, 0, :, columns]

    each_pair(move)


def to_blocks(rows, parts):
    arrays, _, tokens, features = rows.shape
    return pl.pallas_call(
        to_blocks_kernel,
        out_shape=jax.ShapeDtypeStruct((parts, arrays, tokens, features // parts), rows.dtype),
        in_specs=[VMEM],
        out_specs=VMEM,
        compiler_params=PARAMS,
        cost_estimate=pl.CostEstimate(flops=0, bytes_accessed=4 * rows.size, transcendentals=0),
    )(rows)


def to_rows_kernel(blocks_ref, rows_ref):
    parts, _, width = blocks_ref.shape

    def move(pair):
        for part in range(parts):
            target = (part + pair * parts // 2) % parts
            rows_ref[0, :, target * width : (target + 1) * width] = blocks_ref[part]

    each_pair(move)


def to_rows(blocks):
    parts, tokens, width = blocks.shape
    return pl.pallas_call(
        to_rows_kernel,
        out_shape=jax.ShapeDtypeStruct((1, tokens, parts * width), blocks.dtype),
        in_specs=[VMEM],
        out_specs=VMEM,
        compiler_params=PARAMS,
        cost_estimate=pl.CostEstimate(flops=0, bytes_accessed=4 * blocks.size, transcendentals=0),
    )(blocks)


def columns_of(pieces, head):
    rows = pieces[:, :, head * HEAD_DIM : (head + 1) * HEAD_DIM]
    return rows.reshape(rows.shape[0] * rows.shape[1], HEAD_DIM)


def key_of(place, head):
    ref, tile = place
    return columns_of(ref.at[tile, :, 0], head)


def value_of(place, head):
    ref, tile = place
    return columns_of(ref.at[tile, :, 1], head)


def lanes(op, score):
    return functools.reduce(
        op, [score[:, k : k + HEAD_DIM] for k in range(0, score.shape[1], HEAD_DIM)]
    )


def score(query, key):
    return lax.dot_general(query, key, (((1,), (1,)), ((), ())), preferred_element_type=jnp.float32)


def attend(q_ref, out_ref, flag_ref, tile, places):
    _, pieces, piece, width = out_ref.shape
    heads = range(width // HEAD_DIM)
    queries = [columns_of(q_ref.at[tile], head) for head in heads]
    ready = [score(queries[0], key_of(place, 0)) for place in places]
    largest = 0.0
    for head in heads:
        scores, ready = ready, []
        shift = jnp.max(lanes(jnp.maximum, scores[0]), axis=1, keepdims=True) * SCALE
        total, mixed = 0.0, 0.0
        for one, place in zip(scores, places):
            weight = jnp.exp2(one * SCALE - shift)
            total += lanes(jnp.add, weight)
            if head + 1 < len(heads):
                ready.append(score(queries[head + 1], key_of(place, head + 1)))
            mixed += jnp.dot(
                weight.astype(jnp.bfloat16),
                value_of(place, head),
                preferred_element_type=jnp.float32,
            )
        largest = jnp.maximum(largest, total)
        mixed = mixed / jnp.sum(total, axis=1, keepdims=True)
        columns = slice(head * HEAD_DIM, (head + 1) * HEAD_DIM)
        out_ref[tile, :, :, columns] = mixed.astype(jnp.bfloat16).reshape(pieces, piece, HEAD_DIM)
    if len(places) > 1:
        flag_ref[0] = jnp.where(jnp.max(largest) < LARGE, 0, 1)


def attend_safely(q_ref, out_ref, tile, asked):
    _, pieces, piece, width = out_ref.shape
    for head in range(width // HEAD_DIM):
        query = columns_of(q_ref.at[tile], head)
        scores = [score(query, key_of(place, head)) for place, _ in asked]
        biases = [jnp.where(allowed, 0.0, BLOCKED) for _, allowed in asked]
        tops = [lanes(jnp.maximum, one) + bias for one, bias in zip(scores, biases)]
        peak = jnp.max(functools.reduce(jnp.maximum, tops), axis=1, keepdims=True)
        total, mixed = 0.0, 0.0
        for one, bias, (place, _) in zip(scores, biases, asked):
            weight = jnp.exp2(one * SCALE + (bias - peak) * SCALE)
            total += lanes(jnp.add, weight)
            mixed += jnp.dot(
                weight.astype(jnp.bfloat16),
                value_of(place, head),
                preferred_element_type=jnp.float32,
            )
        mixed = mixed / jnp.sum(total, axis=1, keepdims=True)
        columns = slice(head * HEAD_DIM, (head + 1) * HEAD_DIM)
        out_ref[tile, :, :, columns] = mixed.astype(jnp.bfloat16).reshape(pieces, piece, HEAD_DIM)


def attend_kernel(
    pattern_ref, counts_ref, q_ref, own_ref, x_ref, z1_ref, z0_ref, out_ref, flag_ref
):
    tiles = out_ref.shape[0]
    last = counts_ref.shape[0] - 1
    slab, pair = lax.axis_index("slab"), lax.axis_index("pair")
    core = lax.rem(lax.axis_index("head"), 2)
    here = counts_ref[slab]
    below = jnp.where(slab >= 1, counts_ref[jnp.maximum(slab - 1, 0)], 0)
    above = jnp.where(slab < last, counts_ref[jnp.minimum(slab + 1, last)], 0)

    @pl.loop(0, tiles)
    def _(tile):
        slot = tiles * pair + tile
        live = slot < here
        left = pattern_ref[slot, 1] == 1
        right = (pattern_ref[slot, 2] == 1) & (slot + 1 < here)
        down = (pattern_ref[slot, 3] == 1) & (slot < below)
        up = (pattern_ref[slot, 4] == 1) & (slot < above)
        inner, outer = (tile == 0, tile == 1)
        others = [
            ((own_ref, 1 - tile), (inner & right) | (outer & left)),
            ((x_ref, 0), (pair != tile) & ((inner & left) | (outer & right))),
            ((z0_ref, tile), ((core == 0) & down) | ((core == 1) & up)),
            ((z1_ref, tile), ((core == 0) & up) | ((core == 1) & down)),
        ]
        flag_ref[0] = 0
        def choose(k, places):
            if k == len(others):
                attend(q_ref, out_ref, flag_ref, tile, places)
                return
            place, allowed = others[k]
            pl.when(allowed)(lambda: choose(k + 1, places + [place]))
            pl.when(jnp.logical_not(allowed))(lambda: choose(k + 1, places))

        pl.when(live)(lambda: choose(0, [(own_ref, tile)]))

        asked = [((own_ref, tile), True)] + others
        unsafe = live & (flag_ref[0] == 1)
        pl.when(unsafe)(functools.partial(attend_safely, q_ref, out_ref, tile, asked))

        @pl.when(jnp.logical_not(live))
        def _():
            out_ref[tile] = jnp.zeros(out_ref.shape[1:], jnp.bfloat16)


def on_device(qkv, pattern, counts):
    pair_len, heads = lax.axis_size("lane"), lax.axis_size("head")
    parts = pair_len * heads
    piece, features = qkv.shape[2], qkv.shape[3]
    width = features // parts
    pair = lax.axis_index("pair")
    own = spread(to_blocks(qkv[1:3], parts))
    own, raw_query = lax.optimization_barrier((own, to_blocks(qkv[:1], parts)))
    own = own.reshape(pair_len, heads, 2, piece, width)
    z0 = passed_along(own, 1)
    z1 = passed_along(own, -1)
    x = swapped_across(lax.dynamic_slice_in_dim(own, 1 - pair, 1, axis=0))
    query = spread(raw_query).reshape(pair_len, heads, piece, width)
    attended = pl.pallas_call(
        attend_kernel,
        out_shape=jax.ShapeDtypeStruct(query.shape, jnp.bfloat16),
        in_specs=[SMEM] * 2 + [VMEM] * 5,
        out_specs=VMEM,
        scratch_shapes=[pltpu.SMEM((1,), jnp.int32)],
        compiler_params=PARAMS,
        cost_estimate=pl.CostEstimate(flops=10**9, bytes_accessed=2**22, transcendentals=0),
    )(pattern, counts, query, own, x, z1, z0)
    return to_rows(spread(attended.reshape(parts, piece, width)))


def solution(mesh):
    slabs, heads, slots = (mesh.shape[axis] for axis in ("slab", "head", "seq"))
    halves = Mesh(mesh.devices.reshape(slabs, heads, 2, slots // 2), ("slab", "head", "pair", "lane"))
    in_specs = (P(None, ("slab", "pair", "lane"), "head", None), P("slab", None), P())
    out_specs = P(("slab", "pair", "lane"), "head", None)
    return jax.shard_map(
        on_device, mesh=halves, in_specs=in_specs, out_specs=out_specs, check_vma=False
    )
```
